32 devices in a mesh: word: 4 (over x, core), ctx: 8 (over z, y).
Axes of the slice: x: 2, y: 2, z: 4, core: 2. Of those that a mesh axis runs over, the one named last changes fastest.
Arguments:
- counts: int32 [6144, 12288], P('word', 'ctx'), may hold values from 0 to 1800, as said below
- word_vecs: float32 [6144, 300], P(('word', 'ctx')), may hold values from -0.35 to 0.35
- word_bias: float32 [6144], P(('word', 'ctx')), may hold values from 0.5 to 3
- word_accum: float32 [6144, 300], P(('word', 'ctx')), may hold values from 3.2552084e-06 to 0.00016276042
- word_bias_accum: float32 [6144], P(('word', 'ctx')), may hold values from 1 to 30
- ctx_vecs: float32 [12288, 300], P(('ctx', 'word')), may hold values from -0.35 to 0.35
- ctx_bias: float32 [12288], P(('ctx', 'word')), may hold values from 0.5 to 3
- ctx_accum: float32 [12288, 300], P(('ctx', 'word')), may hold values from 6.510417e-06 to 0.00032552084
- ctx_bias_accum: float32 [12288], P(('ctx', 'word')), may hold values from 1 to 30
Outputs:
- new_word_vecs: float32 [6144, 300], P(('word', 'ctx'))
- new_word_bias: float32 [6144], P(('word', 'ctx'))
- new_word_accum: float32 [6144, 300], P(('word', 'ctx'))
- new_word_bias_accum: float32 [6144], P(('word', 'ctx'))
- new_ctx_vecs: float32 [12288, 300], P(('ctx', 'word'))
- new_ctx_bias: float32 [12288], P(('ctx', 'word'))
- new_ctx_accum: float32 [12288, 300], P(('ctx', 'word'))
- new_ctx_bias_accum: float32 [12288], P(('ctx', 'word'))
The draws below stay inside these ranges and needn't reach their ends.
Inputs may be any that keep to these rules, and one draw needn't show every extreme that they name: counts are non-negative integers, and a count is zero exactly where the word and the context never co-occur.
All inputs are finite; a program needn't handle non-finite values.
Results may differ from the reference program's by a relative error of at most 0.0045.
Values may be sent and summed in bfloat16 or wider, within the bound.
A program may use at most 64 MiB of HBM per device.

```python
import math
import jax
import jax.numpy as jnp
from jax import lax

D = 300
TW = 1536
WORDS = 6144
CONTEXTS = 12288


def draw_counts(key, part):
    key_scale = jax.random.fold_in(key, 11)
    key_value = jax.random.fold_in(key, 23)
    key_empty = jax.random.fold_in(key, 37)
    shape = (WORDS, CONTEXTS)
    exponent = jax.random.randint(key_scale, shape, 0, 12)
    upper = jnp.left_shift(jnp.ones(shape, jnp.int32), exponent) + 1
    values = jnp.minimum(jax.random.randint(key_value, shape, 1, upper), 1800)
    empty = jax.random.randint(key_empty, shape, 0, 8) == 0
    drawn = jnp.where(empty, 0, values)
    rows = jnp.arange(WORDS, dtype=jnp.int32)[:, None]
    cols = jnp.arange(CONTEXTS, dtype=jnp.int32)[None, :]
    corner = (rows == 0) & (cols == 0)
    return jnp.where(corner, 1800, drawn).astype(jnp.int32)


def draw_word_vecs(key, part):
    key_entries = jax.random.fold_in(key, 43)
    entries = 0.1 * jax.random.normal(key_entries, (WORDS, D), jnp.float32)
    return jnp.clip(entries, -0.35, 0.35).astype(jnp.float32)


def draw_ctx_vecs(key, part):
    key_entries = jax.random.fold_in(key, 59)
    entries = 0.1 * jax.random.normal(key_entries, (CONTEXTS, D), jnp.float32)
    return jnp.clip(entries, -0.35, 0.35).astype(jnp.float32)


def steps_of(stream_key, dims, pieces, least, top_value):
    def one(dim, parts):
        heights = jax.random.uniform(jax.random.fold_in(jax.random.fold_in(stream_key, 6), dim), (parts,), jnp.float32, least / len(pieces), top_value / len(pieces))
        return jnp.repeat(jnp.exp(heights), dims[dim] // parts).reshape((-1,) + (1,) * (len(dims) - dim - 1))

    factor_of = one(*pieces[0])
    for cut in pieces[1:]:
        factor_of = factor_of * one(*cut)
    return factor_of


def setup_inputs(seed: int = 0) -> dict:
    arg_keys = jax.random.split(jax.random.key(seed), 10)
    return {
        "counts": draw_counts(jax.random.fold_in(arg_keys[9], 71), 0),
        "word_vecs": draw_word_vecs(jax.random.fold_in(arg_keys[9], 71), 0),
        "word_bias": jnp.clip(0.5 + 2.5 * jax.random.uniform(arg_keys[2], (WORDS,), jnp.float32) ** steps_of(arg_keys[2], (WORDS,), ((0, 32),), -0.2, 0.2), 0.5, 3.0),
        "word_accum": jnp.clip(jnp.exp(math.log(0.00016276042) - 3.912023 * jax.random.uniform(arg_keys[3], (WORDS, D), jnp.float32) ** steps_of(arg_keys[3], (WORDS, D), ((0, 32),), -0.2, 0.2)), 3.2552084121562075e-06, 0.00016276042),
        "word_bias_accum": jnp.clip(jnp.exp(math.log(30.0) - 3.4011974 * jax.random.uniform(arg_keys[4], (WORDS,), jnp.float32) ** steps_of(arg_keys[4], (WORDS,), ((0, 32),), -0.2, 0.2)), 1.0, 30.0),
        "ctx_vecs": draw_ctx_vecs(jax.random.fold_in(arg_keys[9], 71), 0),
        "ctx_bias": jnp.clip(0.5 + 2.5 * jax.random.uniform(arg_keys[6], (CONTEXTS,), jnp.float32) ** steps_of(arg_keys[6], (CONTEXTS,), ((0, 32),), -0.2, 0.2), 0.5, 3.0),
        "ctx_accum": jnp.clip(jnp.exp(math.log(0.00032552084) - 3.912023 * jax.random.uniform(arg_keys[7], (CONTEXTS, D), jnp.float32) ** steps_of(arg_keys[7], (CONTEXTS, D), ((0, 32),), -0.2, 0.2)), 6.510416824312415e-06, 0.00032552084),
        "ctx_bias_accum": jnp.clip(jnp.exp(math.log(30.0) - 3.4011974 * jax.random.uniform(arg_keys[8], (CONTEXTS,), jnp.float32) ** steps_of(arg_keys[8], (CONTEXTS,), ((0, 32),), -0.2, 0.2)), 1.0, 30.0),
    }


count_cap = 100.0
power_law = 0.75
step_rate = 0.2

def weighted_residual(tile_counts, word_rows, ctx_rows, word_bias_rows, ctx_bias_rows):
    values = tile_counts.astype(jnp.float32)
    log_count = jnp.log(jnp.maximum(values, 1.0))
    weight = jnp.where(tile_counts > 0, jnp.minimum((values / count_cap) ** power_law, 1.0), 0.0)
    inner = lax.dot_general(word_rows, ctx_rows, (((1,), (1,)), ((), ())), preferred_element_type=jnp.float32)
    return weight * (inner + word_bias_rows[:, None] + ctx_bias_rows[None, :] - log_count)

def adagrad(param, accum, grad):
    new_accum = accum + grad * grad
    return (param - step_rate * grad / jnp.sqrt(new_accum), new_accum)

def reference(counts, word_vecs, word_bias, word_accum, word_bias_accum, ctx_vecs, ctx_bias, ctx_accum, ctx_bias_accum):
    word_low = word_vecs.astype(jnp.bfloat16)
    ctx_low = ctx_vecs.astype(jnp.bfloat16)
    word_bias_f = lax.optimization_barrier(word_bias.astype(jnp.bfloat16)).astype(jnp.float32)
    ctx_bias_f = lax.optimization_barrier(ctx_bias.astype(jnp.bfloat16)).astype(jnp.float32)
    groups = WORDS // TW
    count_blocks = counts.reshape(groups, TW, CONTEXTS)
    word_blocks = word_low.reshape(groups, TW, D)
    bias_blocks = word_bias_f.reshape(groups, TW)

    def one_block(carry, inputs):
        ctx_total, ctx_bias_total = carry
        block_counts, block_words, block_bias = inputs
        scaled = weighted_residual(block_counts, block_words, ctx_low, block_bias, ctx_bias_f)
        scaled_low = scaled.astype(jnp.bfloat16)
        word_term = jnp.dot(scaled_low, ctx_low, preferred_element_type=jnp.float32)
        word_bias_term = lax.optimization_barrier(jnp.sum(scaled, axis=1))
        ctx_term = lax.dot_general(scaled_low, block_words, (((0,), (0,)), ((), ())), preferred_element_type=jnp.float32)
        return ((ctx_total + ctx_term, ctx_bias_total + lax.optimization_barrier(jnp.sum(scaled, axis=0))), (word_term, word_bias_term))
    start = (jnp.zeros((CONTEXTS, D), jnp.float32), jnp.zeros((CONTEXTS,), jnp.float32))
    (ctx_sum, ctx_bias_sum), (word_sum, word_bias_sum) = lax.scan(one_block, start, (count_blocks, word_blocks, bias_blocks))
    word_grad = 2.0 / CONTEXTS * word_sum.reshape(WORDS, D)
    word_bias_grad = 2.0 / CONTEXTS * word_bias_sum.reshape(WORDS)
    ctx_grad = 2.0 / WORDS * ctx_sum
    ctx_bias_grad = 2.0 / WORDS * ctx_bias_sum
    new_word_vecs, new_word_accum = adagrad(word_vecs, word_accum, word_grad)
    new_word_bias, new_word_bias_accum = adagrad(word_bias, word_bias_accum, word_bias_grad)
    new_ctx_vecs, new_ctx_accum = adagrad(ctx_vecs, ctx_accum, ctx_grad)
    new_ctx_bias, new_ctx_bias_accum = adagrad(ctx_bias, ctx_bias_accum, ctx_bias_grad)
    return (new_word_vecs, new_word_bias, new_word_accum, new_word_bias_accum, new_ctx_vecs, new_ctx_bias, new_ctx_accum, new_ctx_bias_accum)
```

```python
import functools
import math

import jax
import jax.numpy as jnp
from jax import lax
from jax.experimental import pallas as pl
from jax.experimental.pallas import tpu as pltpu
from jax.sharding import PartitionSpec as P

count_cap = 100.0
power_law = 0.75
step_rate = 0.2


def weighted_residual(tile_counts, word_rows, ctx_rows, word_bias_rows, ctx_bias_rows):
    values = tile_counts.astype(jnp.float32)
    log_count = jnp.log(jnp.maximum(values, 1.0))
    weight = jnp.where(tile_counts > 0, jnp.minimum((values / count_cap) ** power_law, 1.0), 0.0)
    inner = lax.dot_general(
        word_rows, ctx_rows, (((1,), (1,)), ((), ())), preferred_element_type=jnp.float32
    )
    return weight * (inner + word_bias_rows[:, None] + ctx_bias_rows[None, :] - log_count)


def adagrad(param, accum, grad):
    new_accum = accum + grad * grad
    return (param - step_rate * grad / jnp.sqrt(new_accum), new_accum)


def per_device_plain(
    counts,
    word_vecs,
    word_bias,
    word_accum,
    word_bias_accum,
    ctx_vecs,
    ctx_bias,
    ctx_accum,
    ctx_bias_accum,
):
    word_rows, word_bias_rows = (
        lax.all_gather(word_vecs.astype(jnp.bfloat16), "ctx", axis=0, tiled=True),
        lax.all_gather(word_bias.astype(jnp.bfloat16), "ctx", axis=0, tiled=True),
    )
    ctx_rows, ctx_bias_rows = (
        lax.all_gather(ctx_vecs.astype(jnp.bfloat16), "word", axis=0, tiled=True),
        lax.all_gather(ctx_bias.astype(jnp.bfloat16), "word", axis=0, tiled=True),
    )
    scaled = weighted_residual(
        counts,
        word_rows,
        ctx_rows,
        word_bias_rows.astype(jnp.float32),
        ctx_bias_rows.astype(jnp.float32),
    )
    scaled_low = scaled.astype(jnp.bfloat16)
    word_term = jnp.dot(scaled_low, ctx_rows, preferred_element_type=jnp.float32)
    word_bias_term = jnp.sum(scaled, axis=1)
    ctx_term = lax.dot_general(
        scaled_low, word_rows, (((0,), (0,)), ((), ())), preferred_element_type=jnp.float32
    )
    ctx_bias_term = jnp.sum(scaled, axis=0)
    word_sum, word_bias_sum = (
        lax.psum_scatter(word_term, "ctx", scatter_dimension=0, tiled=True),
        lax.psum_scatter(word_bias_term, "ctx", scatter_dimension=0, tiled=True),
    )
    ctx_sum, ctx_bias_sum = (
        lax.psum_scatter(ctx_term, "word", scatter_dimension=0, tiled=True),
        lax.psum_scatter(ctx_bias_term, "word", scatter_dimension=0, tiled=True),
    )
    all_contexts = counts.shape[1] * lax.axis_size("ctx")
    all_words = counts.shape[0] * lax.axis_size("word")
    word_scale = 2.0 / all_contexts
    ctx_scale = 2.0 / all_words
    new_word_vecs, new_word_accum = adagrad(word_vecs, word_accum, word_scale * word_sum)
    new_word_bias, new_word_bias_accum = adagrad(
        word_bias, word_bias_accum, word_scale * word_bias_sum
    )
    new_ctx_vecs, new_ctx_accum = adagrad(ctx_vecs, ctx_accum, ctx_scale * ctx_sum)
    new_ctx_bias, new_ctx_bias_accum = adagrad(ctx_bias, ctx_bias_accum, ctx_scale * ctx_bias_sum)
    return (
        new_word_vecs,
        new_word_bias,
        new_word_accum,
        new_word_bias_accum,
        new_ctx_vecs,
        new_ctx_bias,
        new_ctx_accum,
        new_ctx_bias_accum,
    )


MESH = pl.DeviceIdType.MESH


def remote(src, dst, send_sem, recv_sem, device):
    return pltpu.make_async_remote_copy(
        src_ref=src,
        dst_ref=dst,
        send_sem=send_sem,
        recv_sem=recv_sem,
        device_id=device,
        device_id_type=MESH,
    )


def near_first(n):
    return sorted(range(n), key=lambda d: (min(d, n - d), d))


def tile_kernel(
    n_word,
    n_ctx,
    counts_hbm,
    word_own,
    ctx_own,
    word_out,
    ctx_out,
    counts,
    weight,
    log_count,
    scaled_low,
    word_all,
    word_all_t,
    ctx_all,
    own_part,
    y_out,
    y_in,
    z_out,
    z_in,
    ctx_part,
    core_out,
    core_in,
    x_out,
    x_in,
    count_sem,
    wz_s,
    wz_r,
    wy_s,
    wy_r,
    cx_s,
    cx_r,
    cc_s,
    cc_r,
    ry_s,
    ry_r,
    rz_s,
    rz_r,
    rc_s,
    rc_r,
    rx_s,
    rx_r,
):
    rows, lanes = word_own.shape
    depth, cols = ctx_own.shape
    nz, nx = n_ctx // 2, n_word // 2
    w, c = lax.axis_index("word"), lax.axis_index("ctx")
    x, core = w // 2, w % 2
    z, y = c // 2, c % 2

    def ctx_peer(zi, yi):
        return (w, zi * 2 + yi)

    def word_peer(xi, ci):
        return (xi * 2 + ci, c)

    def zf(d):
        return (z + d) % nz

    def zb(d):
        return (z + nz - d) % nz

    def xf(d):
        return (x + d) % nx

    def xb(d):
        return (x + nx - d) % nx

    def word_rows(block):
        return pl.ds(pl.multiple_of(block * rows, rows), rows)

    def ctx_cols(block):
        return pl.ds(pl.multiple_of(block * cols, cols), cols)

    z_order = near_first(nz)
    steps = []
    for i, d in enumerate(z_order):
        pair = [(d, True), (d, False)]
        steps += pair if i < 2 else pair[::-1]

    def block_of(step):
        d, mine = step
        return zb(d) * 2 + (y if mine else 1 - y)

    count_copies = []
    for i, step in enumerate(steps):
        at = word_rows(block_of(step))
        copy = pltpu.make_async_copy(counts_hbm.at[at, :], counts.at[at, :], count_sem.at[i])
        copy.start()
        count_copies.append(copy)

    barrier = pltpu.get_barrier_semaphore()
    peers = [ctx_peer(zf(d), y) for d in range(1, nz)] + [ctx_peer(z, 1 - y)]
    peers += [word_peer(xf(d), core) for d in range(1, nx)] + [word_peer(x, 1 - core)]
    for peer in peers:
        pl.semaphore_signal(barrier, inc=1, device_id=peer, device_id_type=MESH)
    pl.semaphore_wait(barrier, len(peers))

    sends = []
    wz, wy, cx, cc = {}, {}, {}, {}

    def wy_copy(d, src):
        at = word_rows(zb(d) * 2 + y)
        wy[d] = remote(src, word_all.at[at, :], wy_s.at[d], wy_r.at[d], ctx_peer(z, 1 - y))
        wy[d].start()
        sends.append(wy[d])

    def cc_copy(d, src):
        at = ctx_cols(xb(d) * 2 + core)
        cc[d] = remote(
            src, ctx_all.at[:depth, at], cc_s.at[d], cc_r.at[d], word_peer(x, 1 - core)
        )
        cc[d].start()
        sends.append(cc[d])

    for d in range(1, nx):
        cx[d] = remote(
            ctx_own,
            ctx_all.at[:depth, ctx_cols(w)],
            cx_s.at[d - 1],
            cx_r.at[d - 1],
            word_peer(xf(d), core),
        )
        cx[d].start()
        sends.append(cx[d])
    cc_copy(0, ctx_own)
    wy_copy(0, word_own)
    for d in z_order[1:]:
        wz[d] = remote(
            word_own,
            word_all.at[word_rows(c), :],
            wz_s.at[d - 1],
            wz_r.at[d - 1],
            ctx_peer(zf(d), y),
        )
        wz[d].start()
        sends.append(wz[d])
    word_all[word_rows(c), :] = word_own[...]
    ctx_all[:depth, ctx_cols(w)] = ctx_own[...]
    ctx_all[depth:, :] = jnp.zeros((lanes - depth, ctx_all.shape[1]), ctx_all.dtype)

    forwards = [("c", d) for d in range(1, nx)] + [("w", d) for d in z_order[1:]]

    def forward():
        if not forwards:
            return
        kind, d = forwards.pop(0)
        if kind == "c":
            cx[d].wait_recv()
            cc_copy(d, ctx_all.at[:depth, ctx_cols(xb(d) * 2 + core)])
        else:
            wz[d].wait_recv()
            wy_copy(d, word_all.at[word_rows(zb(d) * 2 + y), :])

    group = 16
    log2_cap = math.log2(count_cap)
    for i, step in enumerate(steps):
        count_copies[i].wait()
        base = block_of(step) * rows

        @pl.loop(0, rows // group)
        def _(r):
            at = pl.ds(pl.multiple_of(base + r * group, group), group)
            tile = counts[at, :]
            log2 = jnp.log2(jnp.maximum(tile.astype(jnp.float32), 1.0))
            power = jnp.minimum(jnp.exp2(power_law * (log2 - log2_cap)), 1.0)
            weight[at, :] = jnp.where(tile > 0, power, 0.0)
            log_count[at, :] = log2 * math.log(2.0)

        if i >= 2:
            forward()
    while forwards:
        forward()
    for d in range(nx):
        cc[d].wait_recv()

    ry, rz, rc, rx = {}, {}, {}, {}
    wait_combine = []

    def combine(d):
        ry[d].wait_recv()
        total = own_part[d] + y_in[d].astype(jnp.float32)
        if d == 0:
            own_part[d] = total
        else:
            z_out[d - 1] = total.astype(jnp.bfloat16)
            rz[d] = remote(
                z_out.at[d - 1],
                z_in.at[d - 1],
                rz_s.at[d - 1],
                rz_r.at[d - 1],
                ctx_peer(zb(d), y),
            )
            rz[d].start()
            sends.append(rz[d])

    done = set()
    for step in steps:
        d, mine = step
        at = word_rows(block_of(step))
        if not mine:
            wy[d].wait_recv()
        block = word_all[at, :]
        for j in range(n_word):
            part = pl.ds(j * cols, cols)
            inner = jnp.dot(block, ctx_all[:, part], preferred_element_type=jnp.float32)
            scaled = weight[at, part] * (inner - log_count[at, part])
            scaled_low[at, part] = scaled.astype(jnp.bfloat16)
        term = lax.dot_general(
            scaled_low[at, :],
            ctx_all[...],
            (((1,), (1,)), ((), ())),
            preferred_element_type=jnp.float32,
        )
        if mine:
            own_part[d] = term
        else:
            y_out[d] = term.astype(jnp.bfloat16)
            ry[d] = remote(
                y_out.at[d], y_in.at[d], ry_s.at[d], ry_r.at[d], ctx_peer(z, 1 - y)
            )
            ry[d].start()
            sends.append(ry[d])
        if wait_combine and d != wait_combine[0]:
            combine(wait_combine.pop(0))
        done.add(step)
        if (d, True) in done and (d, False) in done:
            wait_combine.append(d)

    all_rows = word_all.shape[0]
    chunk = 128
    for k in range(0, all_rows, chunk):
        piece = word_all[k : k + chunk, :].astype(jnp.float32)
        word_all_t[:, k : k + chunk] = piece.T.astype(jnp.bfloat16)

    def ctx_term(block):
        return jnp.dot(
            word_all_t[:depth, :],
            scaled_low[:, ctx_cols(block)],
            preferred_element_type=jnp.float32,
        )

    for d in list(range(1, nx)) + [0]:
        core_out[d] = ctx_term(xb(d) * 2 + 1 - core).astype(jnp.bfloat16)
        rc[d] = remote(
            core_out.at[d], core_in.at[d], rc_s.at[d], rc_r.at[d], word_peer(x, 1 - core)
        )
        rc[d].start()
        sends.append(rc[d])
        if wait_combine:
            combine(wait_combine.pop(0))
        ctx_part[...] = ctx_term(xb(d) * 2 + core)
        rc[d].wait_recv()
        total = ctx_part[...] + core_in[d].astype(jnp.float32)
        if d == 0:
            ctx_part[...] = total
        else:
            x_out[d - 1] = total.astype(jnp.bfloat16)
            rx[d] = remote(
                x_out.at[d - 1],
                x_in.at[d - 1],
                rx_s.at[d - 1],
                rx_r.at[d - 1],
                word_peer(xb(d), core),
            )
            rx[d].start()
            sends.append(rx[d])
    while wait_combine:
        combine(wait_combine.pop(0))

    total = ctx_part[...]
    for d in range(1, nx):
        rx[d].wait_recv()
        total = total + x_in[d - 1].astype(jnp.float32)
    ctx_out[...] = total
    total = own_part[0]
    for d in z_order[1:]:
        rz[d].wait_recv()
        total = total + z_in[d - 1].astype(jnp.float32)
    word_out[...] = total
    for copy in sends:
        copy.wait_send()


def per_device(
    counts,
    word_vecs,
    word_bias,
    word_accum,
    word_bias_accum,
    ctx_vecs,
    ctx_bias,
    ctx_accum,
    ctx_bias_accum,
):
    n_word, n_ctx = lax.axis_size("word"), lax.axis_size("ctx")
    rows, d = word_vecs.shape
    cols = ctx_vecs.shape[0]
    lanes = -(-(d + 2) // 128) * 128
    depth = -(-(d + 2) // 16) * 16
    nz, nx = n_ctx // 2, n_word // 2
    low = jnp.bfloat16
    word_own = jnp.concatenate(
        [
            word_vecs.astype(low),
            word_bias.astype(low)[:, None],
            jnp.ones((rows, 1), low),
            jnp.zeros((rows, lanes - d - 2), low),
        ],
        axis=1,
    )
    ctx_own = jnp.concatenate(
        [
            ctx_vecs.T.astype(low),
            jnp.ones((1, cols), low),
            ctx_bias.astype(low)[None, :],
            jnp.zeros((depth - d - 2, cols), low),
        ],
        axis=0,
    )
    tile_rows, tile_cols = counts.shape
    dma = pltpu.SemaphoreType.DMA
    vmem = pl.BlockSpec(memory_space=pltpu.VMEM)
    word_sum, ctx_sum_t = pl.pallas_call(
        functools.partial(tile_kernel, n_word, n_ctx),
        out_shape=(
            jax.ShapeDtypeStruct((rows, lanes), jnp.float32),
            jax.ShapeDtypeStruct((depth, cols), jnp.float32),
        ),
        in_specs=[pl.BlockSpec(memory_space=pl.ANY), vmem, vmem],
        out_specs=(vmem, vmem),
        scratch_shapes=[
            pltpu.VMEM((tile_rows, tile_cols), jnp.int32),
            pltpu.VMEM((tile_rows, tile_cols), jnp.float32),
            pltpu.VMEM((tile_rows, tile_cols), jnp.float32),
            pltpu.VMEM((tile_rows, tile_cols), low),
            pltpu.VMEM((tile_rows, lanes), low),
            pltpu.VMEM((lanes, tile_rows), low),
            pltpu.VMEM((lanes, tile_cols), low),
            pltpu.VMEM((nz, rows, lanes), jnp.float32),
            pltpu.VMEM((nz, rows, lanes), low),
            pltpu.VMEM((nz, rows, lanes), low),
            pltpu.VMEM((nz - 1, rows, lanes), low),
            pltpu.VMEM((nz - 1, rows, lanes), low),
            pltpu.VMEM((depth, cols), jnp.float32),
            pltpu.VMEM((nx, depth, cols), low),
            pltpu.VMEM((nx, depth, cols), low),
            pltpu.VMEM((nx - 1, depth, cols), low),
            pltpu.VMEM((nx - 1, depth, cols), low),
            dma((n_ctx,)),
            dma((nz - 1,)),
            dma((nz - 1,)),
            dma((nz,)),
            dma((nz,)),
            dma((nx - 1,)),
            dma((nx - 1,)),
            dma((nx,)),
            dma((nx,)),
            dma((nz,)),
            dma((nz,)),
            dma((nz - 1,)),
            dma((nz - 1,)),
            dma((nx,)),
            dma((nx,)),
            dma((nx - 1,)),
            dma((nx - 1,)),
        ],
        compiler_params=pltpu.CompilerParams(
            collective_id=0, has_side_effects=True, vmem_limit_bytes=56 * 2**20
        ),
    )(counts, word_own, ctx_own)
    word_scale = 2.0 / (tile_cols * n_ctx)
    ctx_scale = 2.0 / (tile_rows * n_word)
    new_word_vecs, new_word_accum = adagrad(word_vecs, word_accum, word_scale * word_sum[:, :d])
    new_word_bias, new_word_bias_accum = adagrad(
        word_bias, word_bias_accum, word_scale * word_sum[:, d]
    )
    new_ctx_vecs, new_ctx_accum = adagrad(ctx_vecs, ctx_accum, ctx_scale * ctx_sum_t[:d, :].T)
    new_ctx_bias, new_ctx_bias_accum = adagrad(
        ctx_bias, ctx_bias_accum, ctx_scale * ctx_sum_t[d + 1, :]
    )
    return (
        new_word_vecs,
        new_word_bias,
        new_word_accum,
        new_word_bias_accum,
        new_ctx_vecs,
        new_ctx_bias,
        new_ctx_accum,
        new_ctx_bias_accum,
    )


def fits_kernel(counts, word_vecs, ctx_vecs, mesh):
    n_word, n_ctx = mesh.shape["word"], mesh.shape["ctx"]
    rows = word_vecs.shape[0] // (n_word * n_ctx)
    cols = ctx_vecs.shape[0] // (n_word * n_ctx)
    paired = n_word % 2 == 0 and n_ctx % 2 == 0 and n_word >= 4 and n_ctx >= 4
    return paired and rows % 16 == 0 and cols % 128 == 0


def solution(mesh):
    def whole(counts, word_vecs, word_bias, word_accum, word_bias_accum, ctx_vecs, *rest):
        body = per_device if fits_kernel(counts, word_vecs, ctx_vecs, mesh) else per_device_plain
        return mapped(mesh, body)(
            counts, word_vecs, word_bias, word_accum, word_bias_accum, ctx_vecs, *rest
        )

    return whole


def mapped(mesh, body):
    return jax.shard_map(
        body,
        mesh=mesh,
        in_specs=(
            P("word", "ctx"),
            P(("word", "ctx"), None),
            P(("word", "ctx")),
            P(("word", "ctx"), None),
            P(("word", "ctx")),
            P(("ctx", "word"), None),
            P(("ctx", "word")),
            P(("ctx", "word"), None),
            P(("ctx", "word")),
        ),
        out_specs=(
            P(("word", "ctx"), None),
            P(("word", "ctx")),
            P(("word", "ctx"), None),
            P(("word", "ctx")),
            P(("ctx", "word"), None),
            P(("ctx", "word")),
            P(("ctx", "word"), None),
            P(("ctx", "word")),
        ),
        check_vma=False,
    )
```

```python
import functools
import math

import jax
import jax.numpy as jnp
from jax import lax
from jax.experimental import pallas as pl
from jax.experimental.pallas import tpu as pltpu
from jax.sharding import PartitionSpec as P

count_cap = 100.0
power_law = 0.75
step_rate = 0.2


def weighted_residual(tile_counts, word_rows, ctx_rows, word_bias_rows, ctx_bias_rows):
    values = tile_counts.astype(jnp.float32)
    log_count = jnp.log(jnp.maximum(values, 1.0))
    weight = jnp.where(tile_counts > 0, jnp.minimum((values / count_cap) ** power_law, 1.0), 0.0)
    inner = lax.dot_general(
        word_rows, ctx_rows, (((1,), (1,)), ((), ())), preferred_element_type=jnp.float32
    )
    return weight * (inner + word_bias_rows[:, None] + ctx_bias_rows[None, :] - log_count)


def adagrad(param, accum, grad):
    new_accum = accum + grad * grad
    return (param - step_rate * grad / jnp.sqrt(new_accum), new_accum)


def per_device_plain(
    counts,
    word_vecs,
    word_bias,
    word_accum,
    word_bias_accum,
    ctx_vecs,
    ctx_bias,
    ctx_accum,
    ctx_bias_accum,
):
    word_rows, word_bias_rows = (
        lax.all_gather(word_vecs.astype(jnp.bfloat16), "ctx", axis=0, tiled=True),
        lax.all_gather(word_bias.astype(jnp.bfloat16), "ctx", axis=0, tiled=True),
    )
    ctx_rows, ctx_bias_rows = (
        lax.all_gather(ctx_vecs.astype(jnp.bfloat16), "word", axis=0, tiled=True),
        lax.all_gather(ctx_bias.astype(jnp.bfloat16), "word", axis=0, tiled=True),
    )
    scaled = weighted_residual(
        counts,
        word_rows,
        ctx_rows,
        word_bias_rows.astype(jnp.float32),
        ctx_bias_rows.astype(jnp.float32),
    )
    scaled_low = scaled.astype(jnp.bfloat16)
    word_term = jnp.dot(scaled_low, ctx_rows, preferred_element_type=jnp.float32)
    word_bias_term = jnp.sum(scaled, axis=1)
    ctx_term = lax.dot_general(
        scaled_low, word_rows, (((0,), (0,)), ((), ())), preferred_element_type=jnp.float32
    )
    ctx_bias_term = jnp.sum(scaled, axis=0)
    word_sum, word_bias_sum = (
        lax.psum_scatter(word_term, "ctx", scatter_dimension=0, tiled=True),
        lax.psum_scatter(word_bias_term, "ctx", scatter_dimension=0, tiled=True),
    )
    ctx_sum, ctx_bias_sum = (
        lax.psum_scatter(ctx_term, "word", scatter_dimension=0, tiled=True),
        lax.psum_scatter(ctx_bias_term, "word", scatter_dimension=0, tiled=True),
    )
    all_contexts = counts.shape[1] * lax.axis_size("ctx")
    all_words = counts.shape[0] * lax.axis_size("word")
    word_scale = 2.0 / all_contexts
    ctx_scale = 2.0 / all_words
    new_word_vecs, new_word_accum = adagrad(word_vecs, word_accum, word_scale * word_sum)
    new_word_bias, new_word_bias_accum = adagrad(
        word_bias, word_bias_accum, word_scale * word_bias_sum
    )
    new_ctx_vecs, new_ctx_accum = adagrad(ctx_vecs, ctx_accum, ctx_scale * ctx_sum)
    new_ctx_bias, new_ctx_bias_accum = adagrad(ctx_bias, ctx_bias_accum, ctx_scale * ctx_bias_sum)
    return (
        new_word_vecs,
        new_word_bias,
        new_word_accum,
        new_word_bias_accum,
        new_ctx_vecs,
        new_ctx_bias,
        new_ctx_accum,
        new_ctx_bias_accum,
    )


MESH = pl.DeviceIdType.MESH


def remote(src, dst, send_sem, recv_sem, device):
    return pltpu.make_async_remote_copy(
        src_ref=src,
        dst_ref=dst,
        send_sem=send_sem,
        recv_sem=recv_sem,
        device_id=device,
        device_id_type=MESH,
    )


def near_first(n):
    return sorted(range(n), key=lambda d: (min(d, n - d), d))


def tile_kernel(
    n_word,
    n_ctx,
    counts_hbm,
    word_vecs,
    word_bias,
    ctx_vecs_t,
    ctx_bias,
    word_out,
    ctx_out,
    counts,
    weight,
    log_count,
    scaled_low,
    word_all,
    word_all_t,
    ctx_all,
    own_part,
    y_out,
    y_in,
    z_out,
    z_in,
    ctx_part,
    core_out,
    core_in,
    x_out,
    x_in,
    count_sem,
    wz_s,
    wz_r,
    wy_s,
    wy_r,
    cx_s,
    cx_r,
    cc_s,
    cc_r,
    ry_s,
    ry_r,
    rz_s,
    rz_r,
    rc_s,
    rc_r,
    rx_s,
    rx_r,
):
    rows, lanes = word_out.shape
    depth, cols = ctx_out.shape
    dim = word_vecs.shape[1]
    nz, nx = n_ctx // 2, n_word // 2
    w, c = lax.axis_index("word"), lax.axis_index("ctx")
    x, core = w // 2, w % 2
    z, y = c // 2, c % 2

    def ctx_peer(zi, yi):
        return (w, zi * 2 + yi)

    def word_peer(xi, ci):
        return (xi * 2 + ci, c)

    def zf(d):
        return (z + d) % nz

    def zb(d):
        return (z + nz - d) % nz

    def xf(d):
        return (x + d) % nx

    def xb(d):
        return (x + nx - d) % nx

    def word_rows(block):
        return pl.ds(pl.multiple_of(block * rows, rows), rows)

    def ctx_cols(block):
        return pl.ds(pl.multiple_of(block * cols, cols), cols)

    z_order = near_first(nz)
    steps = []
    for i, d in enumerate(z_order):
        pair = [(d, True), (d, False)]
        steps += pair if i < 2 else pair[::-1]

    def block_of(step):
        d, mine = step
        return zb(d) * 2 + (y if mine else 1 - y)

    count_copies = []
    for i, step in enumerate(steps):
        at = word_rows(block_of(step))
        copy = pltpu.make_async_copy(counts_hbm.at[at, :], counts.at[at, :], count_sem.at[i])
        copy.start()
        count_copies.append(copy)

    barrier = pltpu.get_barrier_semaphore()
    peers = [ctx_peer(zf(d), y) for d in range(1, nz)] + [ctx_peer(z, 1 - y)]
    peers += [word_peer(xf(d), core) for d in range(1, nx)] + [word_peer(x, 1 - core)]
    for peer in peers:
        pl.semaphore_signal(barrier, inc=1, device_id=peer, device_id_type=MESH)
    base = dim // 128 * 128
    at_own = word_rows(c)
    lane = lax.broadcasted_iota(jnp.int32, (rows, lanes - base), 1) + base
    column = jnp.broadcast_to(word_bias[...], (128, rows)).T
    own_part[0, :, base:] = jnp.where(lane == dim, column, jnp.where(lane == dim + 1, 1.0, 0.0))
    own_part[0, :, :dim] = word_vecs[...]
    word_all[at_own, :] = own_part[0].astype(jnp.bfloat16)
    ctx_part[:dim, :] = ctx_vecs_t[...]
    ctx_part[dim : dim + 1, :] = jnp.ones((1, cols), jnp.float32)
    ctx_part[dim + 1 : dim + 2, :] = ctx_bias[...]
    ctx_part[dim + 2 :, :] = jnp.zeros((depth - dim - 2, cols), jnp.float32)
    ctx_all[:depth, ctx_cols(w)] = ctx_part[...].astype(jnp.bfloat16)
    ctx_all[depth:, :] = jnp.zeros((lanes - depth, ctx_all.shape[1]), ctx_all.dtype)
    word_own = word_all.at[at_own, :]
    ctx_own = ctx_all.at[:depth, ctx_cols(w)]

    pl.semaphore_wait(barrier, len(peers))

    sends = []
    wz, wy, cx, cc = {}, {}, {}, {}

    def wy_copy(d, src):
        at = word_rows(zb(d) * 2 + y)
        wy[d] = remote(src, word_all.at[at, :], wy_s.at[d], wy_r.at[d], ctx_peer(z, 1 - y))
        wy[d].start()
        sends.append(wy[d])

    def cc_copy(d, src):
        at = ctx_cols(xb(d) * 2 + core)
        cc[d] = remote(
            src, ctx_all.at[:depth, at], cc_s.at[d], cc_r.at[d], word_peer(x, 1 - core)
        )
        cc[d].start()
        sends.append(cc[d])

    for d in range(1, nx):
        cx[d] = remote(
            ctx_own,
            ctx_all.at[:depth, ctx_cols(w)],
            cx_s.at[d - 1],
            cx_r.at[d - 1],
            word_peer(xf(d), core),
        )
        cx[d].start()
        sends.append(cx[d])
    cc_copy(0, ctx_own)
    wy_copy(0, word_own)
    for d in z_order[1:]:
        wz[d] = remote(
            word_own,
            word_all.at[word_rows(c), :],
            wz_s.at[d - 1],
            wz_r.at[d - 1],
            ctx_peer(zf(d), y),
        )
        wz[d].start()
        sends.append(wz[d])

    def forward_word(d):
        wz[d].wait_recv()
        wy_copy(d, word_all.at[word_rows(zb(d) * 2 + y), :])

    group = 16
    log2_cap = math.log2(count_cap)
    for i, step in enumerate(steps):
        count_copies[i].wait()
        base = block_of(step) * rows

        @pl.loop(0, rows // group)
        def _(r):
            at = pl.ds(pl.multiple_of(base + r * group, group), group)
            tile = counts[at, :]
            log2 = jnp.log2(jnp.maximum(tile.astype(jnp.float32), 1.0))
            power = jnp.minimum(jnp.exp2(power_law * (log2 - log2_cap)), 1.0)
            weight[at, :] = jnp.where(tile > 0, power, 0.0)
            log_count[at, :] = log2 * math.log(2.0)

        if i == len(steps) // 2:
            for d in range(1, nx):
                cx[d].wait_recv()
                cc_copy(d, ctx_all.at[:depth, ctx_cols(xb(d) * 2 + core)])
    forward_word(z_order[1])
    pending = z_order[2:]
    for d in range(nx):
        cc[d].wait_recv()

    ry, rz, rc, rx = {}, {}, {}, {}
    wait_combine = []

    def combine(d):
        ry[d].wait_recv()
        total = own_part[d] + y_in[d].astype(jnp.float32)
        if d == 0:
            own_part[d] = total
        else:
            z_out[d - 1] = total.astype(jnp.bfloat16)
            rz[d] = remote(
                z_out.at[d - 1],
                z_in.at[d - 1],
                rz_s.at[d - 1],
                rz_r.at[d - 1],
                ctx_peer(zb(d), y),
            )
            rz[d].start()
            sends.append(rz[d])

    done = set()
    for step in steps:
        d, mine = step
        at = word_rows(block_of(step))
        if pending and len(done) >= 1:
            forward_word(pending.pop(0))
        if not mine:
            wy[d].wait_recv()
        block = word_all[at, :]
        for j in range(n_word):
            part = pl.ds(j * cols, cols)
            inner = jnp.dot(block, ctx_all[:, part], preferred_element_type=jnp.float32)
            scaled = weight[at, part] * (inner - log_count[at, part])
            scaled_low[at, part] = scaled.astype(jnp.bfloat16)
        term = lax.dot_general(
            scaled_low[at, :],
            ctx_all[...],
            (((1,), (1,)), ((), ())),
            preferred_element_type=jnp.float32,
        )
        if mine:
            own_part[d] = term
        else:
            y_out[d] = term.astype(jnp.bfloat16)
            ry[d] = remote(
                y_out.at[d], y_in.at[d], ry_s.at[d], ry_r.at[d], ctx_peer(z, 1 - y)
            )
            ry[d].start()
            sends.append(ry[d])
        if wait_combine and d != wait_combine[0]:
            combine(wait_combine.pop(0))
        done.add(step)
        if (d, True) in done and (d, False) in done:
            wait_combine.append(d)

    all_rows = word_all.shape[0]
    chunk = 128
    for k in range(0, all_rows, chunk):
        piece = word_all[k : k + chunk, :].astype(jnp.float32)
        word_all_t[:, k : k + chunk] = piece.T.astype(jnp.bfloat16)

    def ctx_term(block):
        return jnp.dot(
            word_all_t[:depth, :],
            scaled_low[:, ctx_cols(block)],
            preferred_element_type=jnp.float32,
        )

    for d in list(range(1, nx)) + [0]:
        core_out[d] = ctx_term(xb(d) * 2 + 1 - core).astype(jnp.bfloat16)
        rc[d] = remote(
            core_out.at[d], core_in.at[d], rc_s.at[d], rc_r.at[d], word_peer(x, 1 - core)
        )
        rc[d].start()
        sends.append(rc[d])
        if wait_combine:
            combine(wait_combine.pop(0))
        ctx_part[...] = ctx_term(xb(d) * 2 + core)
        rc[d].wait_recv()
        total = ctx_part[...] + core_in[d].astype(jnp.float32)
        if d == 0:
            ctx_part[...] = total
        else:
            x_out[d - 1] = total.astype(jnp.bfloat16)
            rx[d] = remote(
                x_out.at[d - 1],
                x_in.at[d - 1],
                rx_s.at[d - 1],
                rx_r.at[d - 1],
                word_peer(xb(d), core),
            )
            rx[d].start()
            sends.append(rx[d])
    while wait_combine:
        combine(wait_combine.pop(0))

    total = ctx_part[...]
    for d in range(1, nx):
        rx[d].wait_recv()
        total = total + x_in[d - 1].astype(jnp.float32)
    ctx_out[...] = total
    total = own_part[0]
    for d in z_order[1:]:
        rz[d].wait_recv()
        total = total + z_in[d - 1].astype(jnp.float32)
    word_out[...] = total
    for copy in sends:
        copy.wait_send()


def update_kernel(word_scale, ctx_scale, word_sum, ctx_sum_t, *refs):
    params, accums, outs = refs[:4], refs[4:8], refs[8:]
    dim = params[0].shape[1]
    base = dim // 128 * 128
    sums = (
        word_scale * word_sum[:, :dim],
        word_scale * word_sum[:, base:].T[dim - base : dim - base + 1, :],
        ctx_scale * ctx_sum_t[:dim, :],
        ctx_scale * ctx_sum_t[dim + 1 : dim + 2, :],
    )
    for i, grad in enumerate(sums):
        outs[i][...], outs[4 + i][...] = adagrad(params[i][...], accums[i][...], grad)


def per_device(
    counts,
    word_vecs,
    word_bias,
    word_accum,
    word_bias_accum,
    ctx_vecs,
    ctx_bias,
    ctx_accum,
    ctx_bias_accum,
):
    n_word, n_ctx = lax.axis_size("word"), lax.axis_size("ctx")
    rows, d = word_vecs.shape
    cols = ctx_vecs.shape[0]
    lanes = -(-(d + 2) // 128) * 128
    depth = -(-(d + 2) // 16) * 16
    nz, nx = n_ctx // 2, n_word // 2
    low = jnp.bfloat16
    tile_rows, tile_cols = counts.shape
    dma = pltpu.SemaphoreType.DMA
    vmem = pl.BlockSpec(memory_space=pltpu.VMEM)
    word_sum, ctx_sum_t = pl.pallas_call(
        functools.partial(tile_kernel, n_word, n_ctx),
        out_shape=(
            jax.ShapeDtypeStruct((rows, lanes), jnp.float32),
            jax.ShapeDtypeStruct((depth, cols), jnp.float32),
        ),
        in_specs=[pl.BlockSpec(memory_space=pl.ANY), vmem, vmem, vmem, vmem],
        out_specs=(vmem, vmem),
        scratch_shapes=[
            pltpu.VMEM((tile_rows, tile_cols), jnp.int32),
            pltpu.VMEM((tile_rows, tile_cols), jnp.float32),
            pltpu.VMEM((tile_rows, tile_cols), jnp.float32),
            pltpu.VMEM((tile_rows, tile_cols), low),
            pltpu.VMEM((tile_rows, lanes), low),
            pltpu.VMEM((lanes, tile_rows), low),
            pltpu.VMEM((lanes, tile_cols), low),
            pltpu.VMEM((nz, rows, lanes), jnp.float32),
            pltpu.VMEM((nz, rows, lanes), low),
            pltpu.VMEM((nz, rows, lanes), low),
            pltpu.VMEM((nz - 1, rows, lanes), low),
            pltpu.VMEM((nz - 1, rows, lanes), low),
            pltpu.VMEM((depth, cols), jnp.float32),
            pltpu.VMEM((nx, depth, cols), low),
            pltpu.VMEM((nx, depth, cols), low),
            pltpu.VMEM((nx - 1, depth, cols), low),
            pltpu.VMEM((nx - 1, depth, cols), low),
            dma((n_ctx,)),
            dma((nz - 1,)),
            dma((nz - 1,)),
            dma((nz,)),
            dma((nz,)),
            dma((nx - 1,)),
            dma((nx - 1,)),
            dma((nx,)),
            dma((nx,)),
            dma((nz,)),
            dma((nz,)),
            dma((nz - 1,)),
            dma((nz - 1,)),
            dma((nx,)),
            dma((nx,)),
            dma((nx - 1,)),
            dma((nx - 1,)),
        ],
        compiler_params=pltpu.CompilerParams(
            collective_id=0, has_side_effects=True, vmem_limit_bytes=56 * 2**20
        ),
    )(counts, word_vecs, word_bias[None, :], ctx_vecs.T, ctx_bias[None, :])
    word_scale = 2.0 / (tile_cols * n_ctx)
    ctx_scale = 2.0 / (tile_rows * n_word)
    shapes = [(rows, d), (1, rows), (d, cols), (1, cols)]
    outs = pl.pallas_call(
        functools.partial(update_kernel, word_scale, ctx_scale),
        out_shape=tuple(jax.ShapeDtypeStruct(shape, jnp.float32) for shape in shapes * 2),
        in_specs=[vmem] * 10,
        out_specs=(vmem,) * 8,
    )(
        word_sum,
        ctx_sum_t,
        word_vecs,
        word_bias[None, :],
        ctx_vecs.T,
        ctx_bias[None, :],
        word_accum,
        word_bias_accum[None, :],
        ctx_accum.T,
        ctx_bias_accum[None, :],
    )
    return (
        outs[0],
        outs[1][0],
        outs[4],
        outs[5][0],
        outs[2].T,
        outs[3][0],
        outs[6].T,
        outs[7][0],
    )


def fits_kernel(counts, word_vecs, ctx_vecs, mesh):
    n_word, n_ctx = mesh.shape["word"], mesh.shape["ctx"]
    rows = word_vecs.shape[0] // (n_word * n_ctx)
    cols = ctx_vecs.shape[0] // (n_word * n_ctx)
    paired = n_word % 2 == 0 and n_ctx % 2 == 0 and n_word >= 4 and n_ctx >= 4
    packed = 0 < word_vecs.shape[1] % 128 <= 126
    return paired and packed and rows % 16 == 0 and cols % 128 == 0


def solution(mesh):
    def whole(counts, word_vecs, word_bias, word_accum, word_bias_accum, ctx_vecs, *rest):
        body = per_device if fits_kernel(counts, word_vecs, ctx_vecs, mesh) else per_device_plain
        return mapped(mesh, body)(
            counts, word_vecs, word_bias, word_accum, word_bias_accum, ctx_vecs, *rest
        )

    return whole


def mapped(mesh, body):
    return jax.shard_map(
        body,
        mesh=mesh,
        in_specs=(
            P("word", "ctx"),
            P(("word", "ctx"), None),
            P(("word", "ctx")),
            P(("word", "ctx"), None),
            P(("word", "ctx")),
            P(("ctx", "word"), None),
            P(("ctx", "word")),
            P(("ctx", "word"), None),
            P(("ctx", "word")),
        ),
        out_specs=(
            P(("word", "ctx"), None),
            P(("word", "ctx")),
            P(("word", "ctx"), None),
            P(("word", "ctx")),
            P(("ctx", "word"), None),
            P(("ctx", "word")),
            P(("ctx", "word"), None),
            P(("ctx", "word")),
        ),
        check_vma=False,
    )
```
